32 devices in a mesh: seq: 8 (over z, y), mp: 4 (over x, core).
Axes of the slice: x: 2, y: 2, z: 4, core: 2. Of those that a mesh axis runs over, the one named last changes fastest.
Arguments:
- token_ids: int32 [2, 1024], P(None, 'seq'), may hold values from 0 to 511, as said below
- pair_mask: int32 [1024], P('seq'), may hold values from 0 to 1
- embed_table: bfloat16 [512, 3, 4096], P(None, None, 'mp'), may hold values from -6 to 6
- conv_filter: bfloat16 [256, 128], P('mp'), may hold values from -0.9 to 1
- w_out: bfloat16 [4096, 4096], P('mp'), may hold values from -0.09375 to 0.09375
- w_qkv: bfloat16 [3, 32, 128, 128], P(None, 'mp'), may hold values from -0.61871843 to 0.61871843
Outputs:
- gram: float32 [32, 128, 128], P('mp', 'seq')
The draws below stay inside these ranges and needn't reach their ends.
Inputs may be any that keep to these rules, and one draw needn't show every extreme that they name: `token_ids`: row 1 equals row 0 at about half of the positions.
All inputs are finite; a program needn't handle non-finite values.
Results may differ from the reference program's by a relative error of at most 0.0074.
Values may be sent and summed in bfloat16 or wider, within the bound.
No kernel may reach another device: no remote copies, remote signals or barrier semaphores. Data moves between devices by JAX's collectives and lax.ppermute only.
A program may use at most 128 MiB of HBM per device.

```python
import math
import jax
import jax.numpy as jnp
from jax import lax

TOK_DEV = 128
HEADS = 32
HEAD = 128
TAPS = 128
GROUP = 16
VOCAB = 512
CHANNELS = 4096
FILTERS = 256
LEN = 1024


def draw_token_ids(key, part):
    key_one, key_two, key_three, key_four = jax.random.split(jax.random.fold_in(key, 11), 4)
    drawn_count = VOCAB - 4
    base_ids = jax.random.randint(key_one, (LEN,), 0, drawn_count, dtype=jnp.int32)
    other_ids = jax.random.randint(key_two, (LEN,), 0, drawn_count, dtype=jnp.int32)
    flipped = jax.random.randint(key_three, (LEN,), 0, 2, dtype=jnp.int32) == 0
    contrast_ids = jnp.where(flipped, other_ids, base_ids)
    spot = jax.random.randint(key_four, (), 0, LEN - 2 * TOK_DEV, dtype=jnp.int32)
    positions = jnp.arange(LEN, dtype=jnp.int32)
    planted = jnp.where(positions == spot, 0, -1)
    planted = jnp.where(positions == LEN - TOK_DEV - 5, VOCAB - 4, planted)
    planted = jnp.where(positions == LEN - TOK_DEV - 1, VOCAB - 3, planted)
    planted = jnp.where(positions == LEN - 2, VOCAB - 2, planted)
    planted = jnp.where(positions == LEN - 1, VOCAB - 1, planted)
    both_rows = jnp.stack([base_ids, contrast_ids])
    return jnp.where(planted[None, :] >= 0, planted[None, :], both_rows).astype(jnp.int32)


def draw_pair_mask(key, part):
    key_one = jax.random.fold_in(key, 17)
    positions = jnp.arange(LEN, dtype=jnp.int32)
    threshold = 200 + 600 * positions // LEN
    picks = jax.random.randint(key_one, (LEN,), 0, 1000, dtype=jnp.int32)
    return (picks < threshold).astype(jnp.int32)


def draw_embed_table(key, part):
    key_one = jax.random.fold_in(jax.random.fold_in(key, 23), 0)
    return jnp.clip(jax.random.normal(key_one, (VOCAB, 3, CHANNELS), jnp.float32), -6.0, 6.0).astype(jnp.bfloat16)


def draw_conv_filter(key, part):
    key_one, key_two, key_three = jax.random.split(jax.random.fold_in(key, 31), 3)
    log_rate = jax.random.uniform(key_one, (FILTERS, 1), jnp.float32, math.log(1.0 / 400.0), math.log(1.0 / 30.0))
    decay_rate = jnp.exp(log_rate)
    lead_tap = jax.random.uniform(key_two, (FILTERS, 1), jnp.float32, 0.3, 1.0)
    lag_index = jnp.arange(TAPS, dtype=jnp.float32)[None, :]
    tail_taps = 0.3 * jnp.clip(jax.random.normal(key_three, (FILTERS, TAPS), jnp.float32), -3.0, 3.0) * jnp.exp(-decay_rate * lag_index)
    return jnp.where(lag_index == 0.0, lead_tap, tail_taps).astype(jnp.bfloat16)


def draw_w_qkv(key, part):
    key_one, key_two, key_three = jax.random.split(jax.random.fold_in(key, 41), 3)
    mat_shape = (HEADS, HEAD, HEAD)
    unit_scale = 1.0 / math.sqrt(HEAD)
    w_query = 1.3 * unit_scale * jnp.clip(jax.random.normal(key_one, mat_shape, jnp.float32), -4.0, 4.0)
    noise_part = 1.3 * unit_scale * jnp.clip(jax.random.normal(key_two, mat_shape, jnp.float32), -4.0, 4.0)
    w_value = unit_scale * jnp.clip(jax.random.normal(key_three, mat_shape, jnp.float32), -4.0, 4.0)
    w_key = noise_part
    return jnp.stack([w_query, w_key, w_value]).astype(jnp.bfloat16)


def shard_levels(rng, extent, pieces, low, top_value):
    factor_of, own = 1.0, jax.random.fold_in(rng, 6)
    for dim, blocks in pieces:
        heights = jnp.exp(jax.random.uniform(jax.random.fold_in(own, dim), (blocks,), jnp.float32, low / len(pieces), top_value / len(pieces)))
        factor_of = factor_of * jnp.repeat(heights, extent[dim] // blocks).reshape([-1 if axis == dim else 1 for axis in range(len(extent))])
    return factor_of


def noise(own_key, shape, deviation, reach, cuts=(), held_as=jnp.bfloat16):
    drawn = jax.random.normal(own_key, shape, jnp.float32) * deviation
    if len(cuts) > 0:
        drawn = shard_levels(own_key, shape, cuts, -0.22, 0.18) * drawn
    return jnp.clip(drawn, min=-reach, max=reach).astype(held_as)


def setup_inputs(seed: int = 0) -> dict:
    streams_of = jax.random.split(jax.random.key(seed), 7)
    token_ids = draw_token_ids(jax.random.fold_in(streams_of[6], 71), 0)
    pair_mask = draw_pair_mask(jax.random.fold_in(streams_of[6], 71), 0)
    embed_table = draw_embed_table(jax.random.fold_in(streams_of[6], 71), 0)
    conv_filter = draw_conv_filter(jax.random.fold_in(streams_of[6], 71), 0)
    w_out = noise(streams_of[4], (CHANNELS, CHANNELS), CHANNELS ** -0.5, 0.09375, ((0, 4),))
    w_qkv = draw_w_qkv(jax.random.fold_in(streams_of[6], 71), 0)
    return {"token_ids": token_ids, "pair_mask": pair_mask, "embed_table": embed_table, "conv_filter": conv_filter, "w_out": w_out, "w_qkv": w_qkv}


MASKED_SCORE = -1e+30

def reference(token_ids, pair_mask, embed_table, conv_filter, w_out, w_qkv):
    features = jnp.take(embed_table, token_ids, axis=0)
    gated = (features[:, :, 1].astype(jnp.float32) * features[:, :, 2].astype(jnp.float32)).astype(jnp.bfloat16)
    tap_table = jnp.repeat(conv_filter.astype(jnp.float32), GROUP, axis=0)
    padded = jnp.pad(gated.astype(jnp.float32), ((0, 0), (TAPS, 0), (0, 0)))

    def add_tap(tap_index, running):
        shifted = lax.dynamic_slice_in_dim(padded, TAPS - tap_index, LEN, 1)
        tap_weight = lax.dynamic_index_in_dim(tap_table, tap_index, 1, keepdims=False)
        return running + shifted * tap_weight[None, None, :]
    convolved = lax.fori_loop(0, TAPS, add_tap, jnp.zeros((2, LEN, CHANNELS), jnp.float32))
    hyena_out = (features[:, :, 0].astype(jnp.float32) * convolved).astype(jnp.bfloat16)
    mixed_out = jnp.dot(hyena_out.reshape(2 * LEN, CHANNELS), w_out, preferred_element_type=jnp.float32)
    mixed_heads = mixed_out.astype(jnp.bfloat16).reshape(2, LEN, HEADS, HEAD).astype(jnp.float32)
    projected = tuple((jnp.einsum('sthd,hde->hste', mixed_heads, w_qkv[which].astype(jnp.float32)).astype(jnp.bfloat16) for which in range(3)))
    mask_float = pair_mask.astype(jnp.float32)
    positions = jnp.arange(LEN, dtype=jnp.int32)
    causal = positions[:, None] >= positions[None, :]
    score_scale = 1.0 / math.sqrt(HEAD)

    def per_head(head_items):
        queries, keys, values = head_items
        scores = jnp.einsum('sqe,ske->sqk', queries.astype(jnp.float32), keys.astype(jnp.float32)) * score_scale
        row_max = lax.optimization_barrier(jnp.max(jnp.where(causal, scores, MASKED_SCORE), axis=-1, keepdims=True))
        weights = jnp.where(causal, jnp.exp(scores - row_max), 0.0)
        row_sum = lax.optimization_barrier(jnp.sum(weights, axis=-1, keepdims=True))
        probs = lax.optimization_barrier(weights.astype(jnp.bfloat16))
        attended = jnp.einsum('sqk,ske->sqe', probs.astype(jnp.float32), values.astype(jnp.float32)) / row_sum
        rounded = lax.optimization_barrier((attended[0] - attended[1]).astype(jnp.bfloat16))
        difference = rounded.astype(jnp.float32)
        kept_rows = difference * mask_float[:, None]
        return jnp.einsum('te,tf->ef', kept_rows, difference)
    gram_sum = lax.map(per_head, projected)
    kept_count = jnp.sum(mask_float)
    return gram_sum / jnp.maximum(kept_count, 1.0)
```

```python
import functools
import math

import jax
import jax.numpy as jnp
from jax import lax
from jax.experimental import pallas as pl
from jax.experimental.pallas import tpu as pltpu
from jax.sharding import PartitionSpec as P

MASKED_SCORE = -1e30
VMEM_BYTES = 24 * 1024 * 1024
TABLES_VMEM_BYTES = 48 * 1024 * 1024
WHOLE = pl.BlockSpec(memory_space=pltpu.VMEM)
IN_HBM = pl.BlockSpec(memory_space=pltpu.HBM)


def params(limit=VMEM_BYTES):
    return pltpu.CompilerParams(vmem_limit_bytes=limit)


def bits_of(count):
    width = count.bit_length() - 1
    assert 1 << width == count
    return width


def swap(value, axis, turn):
    count = lax.axis_size(axis)
    return lax.ppermute(value, axis, [(i, i ^ turn) for i in range(count)])


def gather_small(block, axis):
    index = lax.axis_index(axis)
    held = block[None]
    bits = list(range(bits_of(lax.axis_size(axis))))
    for group in [bits[i : i + 2] for i in range(0, len(bits), 2)]:
        pieces = []
        for turn in range(1 << len(group)):
            mask = turn << group[0]
            pieces.append(held if turn == 0 else swap(held, axis, mask))
        for place, bit in enumerate(group):
            upper = ((index >> bit) & 1) == 1
            pieces = [
                jnp.where(upper, pieces[turn ^ (1 << place)], pieces[turn])
                for turn in range(len(pieces))
            ]
        held = jnp.concatenate(pieces, 0)
    return held


def head_here(seq_count, local_heads):
    return lax.axis_index("seq") // (seq_count // local_heads)


def tables_kernel(
    order, local_heads, seq_count, head_dim, embed_ref, w_out_ref, table_ref, weight_ref, planes,
    columns, plane_sems, column_sems
):
    _, vocab, channels = embed_ref.shape
    chunk = planes.shape[2]
    head = head_here(seq_count, local_heads)
    mp_index = lax.axis_index("mp")
    plane_copies = []
    for c in range(vocab // chunk):
        rows = pl.ds(c * chunk, chunk)
        plane_copies.append(
            [
                pltpu.make_async_copy(embed_ref.at[i, rows], planes.at[i, c], plane_sems.at[i, c])
                for i in range(3)
            ]
        )
    column_copies = []
    for p, turn in enumerate(order):
        first = pl.multiple_of(((mp_index ^ turn) * local_heads + head) * head_dim, head_dim)
        column_copies.append(
            pltpu.make_async_copy(
                w_out_ref.at[:, pl.ds(first, head_dim)], columns.at[p], column_sems.at[p]
            )
        )
    for copy in column_copies:
        copy.start()
    for trio in plane_copies:
        for copy in trio:
            copy.start()
    for p, copy in enumerate(column_copies):
        copy.wait()
        weight_ref[p * head_dim : (p + 1) * head_dim, :] = columns[p].T
    for c, trio in enumerate(plane_copies):
        for copy in trio:
            copy.wait()
        cols = slice(c * chunk, (c + 1) * chunk)
        gated = planes[1, c].astype(jnp.float32) * planes[2, c].astype(jnp.float32)
        table_ref[0:channels, cols] = gated.astype(jnp.bfloat16).T
        table_ref[channels : 2 * channels, cols] = planes[0, c].T


def make_tables(order, seq_count, local_heads, head_dim, embed_rows, w_out):
    _, vocab, channels = embed_rows.shape
    count = len(order)
    chunk = 128
    return pl.pallas_call(
        functools.partial(tables_kernel, order, local_heads, seq_count, head_dim),
        out_shape=[
            jax.ShapeDtypeStruct((2 * channels, vocab), jnp.bfloat16),
            jax.ShapeDtypeStruct((count * head_dim, w_out.shape[0]), jnp.bfloat16),
        ],
        in_specs=[IN_HBM, IN_HBM],
        out_specs=[WHOLE] * 2,
        scratch_shapes=[
            pltpu.VMEM((3, vocab // chunk, chunk, channels), jnp.bfloat16),
            pltpu.VMEM((count, w_out.shape[0], head_dim), jnp.bfloat16),
            pltpu.SemaphoreType.DMA((3, vocab // chunk)),
            pltpu.SemaphoreType.DMA((count,)),
        ],
        compiler_params=params(TABLES_VMEM_BYTES),
        cost_estimate=pl.CostEstimate(
            flops=4 * vocab * channels, bytes_accessed=8 * 1024 * 1024, transcendentals=0
        ),
    )(embed_rows, w_out)


def toeplitz_kernel(filter_ref, toeplitz_ref):
    filters, taps = filter_ref.shape
    row = lax.broadcasted_iota(jnp.int32, (taps, taps), 0)
    col = lax.broadcasted_iota(jnp.int32, (taps, taps), 1)
    for g in range(filters):
        spread = jnp.broadcast_to(filter_ref[g : g + 1, :].astype(jnp.float32), (taps, taps))
        rolled = pltpu.roll(spread, 0, 1, stride=1, stride_axis=0)
        toeplitz_ref[g, 0:taps, :] = jnp.where(col < row, rolled, 0.0).astype(jnp.bfloat16)
        toeplitz_ref[g, taps : 2 * taps, :] = jnp.where(col >= row, rolled, 0.0).astype(
            jnp.bfloat16
        )


def make_toeplitz(conv_filter):
    filters, taps = conv_filter.shape
    return pl.pallas_call(
        toeplitz_kernel,
        out_shape=jax.ShapeDtypeStruct((filters, 2 * taps, taps), jnp.bfloat16),
        in_specs=[WHOLE],
        out_specs=WHOLE,
        compiler_params=params(),
        cost_estimate=pl.CostEstimate(
            flops=4 * filters * taps * taps,
            bytes_accessed=4 * filters * taps * taps,
            transcendentals=0,
        ),
    )(conv_filter)


def hyena_kernel(
    which,
    group,
    ids_ref,
    table_ref,
    toeplitz_ref,
    weight_ref,
    _,
    out_ref,
    pass_ref,
    send_ref,
    feat,
    last,
):
    taps = ids_ref.shape[2]
    channels2, vocab = table_ref.shape
    channels = channels2 // 2
    filters = toeplitz_ref.shape[0]
    blocks = feat.shape[1] // taps
    step_index = pl.program_id(0)

    @pl.when(step_index == 0)
    def _():
        last[...] = jnp.zeros_like(last)

    entry = lax.broadcasted_iota(jnp.int32, (vocab, taps), 0)
    step = 2 if blocks % 2 == 0 else 1
    for b in range(0, blocks, step):
        hot = []
        for j in range(step):
            place = step_index * blocks + b + j
            tokens = jnp.broadcast_to(ids_ref[place, which : which + 1, :], (vocab, taps))
            hot.append((entry == tokens).astype(jnp.float32).astype(jnp.bfloat16))
        feat[:, b * taps : (b + step) * taps] = jnp.dot(
            table_ref[...], jnp.concatenate(hot, axis=1), preferred_element_type=jnp.float32
        ).astype(jnp.bfloat16)

    for g in range(filters):
        rows = slice(g * group, (g + 1) * group)
        lead_rows = slice(channels + g * group, channels + (g + 1) * group)
        tiles = [last[rows, :]] + [feat[rows, b * taps : (b + 1) * taps] for b in range(blocks)]
        window = jnp.concatenate(
            [jnp.concatenate([tiles[b], tiles[b + 1]], axis=1) for b in range(blocks)], axis=0
        )
        conv = jnp.dot(window, toeplitz_ref[g], preferred_element_type=jnp.float32)
        for b in range(blocks):
            cols = slice(b * taps, (b + 1) * taps)
            out_ref[rows, cols] = (
                feat[lead_rows, cols].astype(jnp.float32) * conv[b * group : (b + 1) * group, :]
            ).astype(jnp.bfloat16)
    last[...] = feat[0:channels, (blocks - 1) * taps :]
    rows = send_ref.shape[0]
    total = jnp.dot(weight_ref[2 * rows :, :], out_ref[...], preferred_element_type=jnp.float32)
    pass_ref[...] = total[0:rows]
    send_ref[...] = total[rows:]


def tiles_of(length, taps):
    tile = min(length, 8 * taps)
    assert length % tile == 0
    return tile, length // tile


def column_specs(length, tile, rows):
    if length == tile:
        return [WHOLE for _ in rows]
    return [pl.BlockSpec((count, tile), lambda i: (0, i)) for count in rows]


def hyena(which, group, ids, table, toeplitz, weight, after):
    taps = ids.shape[2]
    channels = table.shape[0] // 2
    vocab = table.shape[1]
    length = ids.shape[0] * taps
    head_dim = weight.shape[0] // 4
    tile, steps = tiles_of(length, taps)
    return pl.pallas_call(
        functools.partial(hyena_kernel, which, group),
        out_shape=[
            jax.ShapeDtypeStruct((channels, length), jnp.bfloat16),
            jax.ShapeDtypeStruct((head_dim, length), jnp.float32),
            jax.ShapeDtypeStruct((head_dim, length), jnp.float32),
        ],
        grid=(steps,),
        in_specs=[WHOLE] * 5,
        out_specs=column_specs(length, tile, (channels, head_dim, head_dim)),
        scratch_shapes=[
            pltpu.VMEM((2 * channels, tile), jnp.bfloat16),
            pltpu.VMEM((channels, taps), jnp.bfloat16),
        ],
        compiler_params=params(),
        cost_estimate=pl.CostEstimate(
            flops=4 * length * channels * (vocab + taps) + 4 * length * channels * head_dim,
            bytes_accessed=8 * 1024 * 1024,
            transcendentals=0,
        ),
    )(ids, table, toeplitz, weight, after)


def project_kernel(mixed_ref, weight_ref, _, own_ref, near_ref):
    rows = own_ref.shape[0]
    total = jnp.dot(
        weight_ref[0 : 2 * rows, :], mixed_ref[...], preferred_element_type=jnp.float32
    )
    own_ref[...] = total[0:rows]
    near_ref[...] = total[rows:]


def project(mixed, weight, taps, after):
    channels, length = mixed.shape
    rows = weight.shape[0] // 4
    tile, steps = tiles_of(length, taps)
    specs = column_specs(length, tile, (channels, rows, rows))
    return pl.pallas_call(
        project_kernel,
        out_shape=[jax.ShapeDtypeStruct((rows, length), jnp.float32)] * 2,
        grid=(steps,),
        in_specs=[specs[0], WHOLE, WHOLE],
        out_specs=specs[1:],
        compiler_params=params(),
        cost_estimate=pl.CostEstimate(
            flops=4 * length * channels * rows, bytes_accessed=1024 * 1024, transcendentals=0
        ),
    )(mixed, weight, after)


def split(exact):
    upper = exact.astype(jnp.bfloat16)
    lower = (exact - upper.astype(jnp.float32)).astype(jnp.bfloat16)
    return jnp.concatenate([upper, lower], axis=0)


def add_kernel(mine_ref, theirs_ref, _, out_ref):
    out_ref[...] = (mine_ref[...] + theirs_ref[...]).astype(out_ref.dtype)


def complete_kernel(own_ref, near_ref, far_ref, mixed_ref):
    mixed_ref[...] = split(own_ref[...] + near_ref[...] + far_ref[...].astype(jnp.float32))


def add_parts(mine, theirs, after):
    return pl.pallas_call(
        add_kernel,
        out_shape=jax.ShapeDtypeStruct(mine.shape, jnp.bfloat16),
        in_specs=[WHOLE] * 3,
        out_specs=WHOLE,
        compiler_params=params(),
        cost_estimate=pl.CostEstimate(
            flops=mine.size, bytes_accessed=10 * mine.size, transcendentals=0
        ),
    )(mine, theirs, after)


def complete(own, near, far):
    rows, length = own.shape
    return pl.pallas_call(
        complete_kernel,
        out_shape=jax.ShapeDtypeStruct((2 * rows, length), jnp.bfloat16),
        in_specs=[WHOLE] * 3,
        out_specs=WHOLE,
        compiler_params=params(),
        cost_estimate=pl.CostEstimate(
            flops=40000 * own.size, bytes_accessed=14 * own.size, transcendentals=0
        ),
    )(own, near, far)


def attend(mixed, w_ref, out_ref):
    head_dim, length = out_ref.shape
    scale = math.log2(math.e) / math.sqrt(head_dim)

    def project_head(which):
        weight = w_ref[which, 0].T
        return jnp.dot(
            jnp.concatenate([weight, weight], axis=1), mixed, preferred_element_type=jnp.float32
        ).astype(jnp.bfloat16)

    queries, keys, values = project_head(0), project_head(1).T, project_head(2)

    def finish(first, parts, values_seen):
        top = functools.reduce(
            jnp.maximum, [jnp.max(part, axis=0, keepdims=True) for part in parts]
        )
        weights = [jnp.exp2((part - top) * scale) for part in parts]
        row_sum = sum(jnp.sum(part, axis=0, keepdims=True) for part in weights)
        probs = jnp.concatenate([part.astype(jnp.bfloat16) for part in weights], axis=0)
        return jnp.dot(values_seen, probs, preferred_element_type=jnp.float32) / row_sum

    def score(keys_seen, queries_block):
        return jnp.dot(keys_seen, queries_block, preferred_element_type=jnp.float32)

    if length <= 2048:
        span = min(512, length)
        row = lax.broadcasted_iota(jnp.int32, (span, span), 0)
        col = lax.broadcasted_iota(jnp.int32, (span, span), 1)
        for first in range(0, length, span):
            cols = slice(first, first + span)
            parts = [jnp.where(row <= col, score(keys[cols], queries[:, cols]), MASKED_SCORE)]
            if first > 0:
                parts = [score(keys[:first], queries[:, cols])] + parts
            out_ref[:, cols] = finish(first, parts, values[:, : first + span])
    else:
        span = 256
        out_ref[...] = queries.astype(jnp.float32)

        @pl.loop(0, length // span)
        def _(i):
            first = pl.multiple_of(i * span, span)
            cols = pl.ds(first, span)
            scores = score(keys, out_ref[:, cols].astype(jnp.bfloat16))
            key_pos = lax.broadcasted_iota(jnp.int32, scores.shape, 0)
            query_pos = first + lax.broadcasted_iota(jnp.int32, scores.shape, 1)
            scores = jnp.where(key_pos <= query_pos, scores, MASKED_SCORE)
            out_ref[:, cols] = finish(first, [scores], values)


def first_kernel(mixed_ref, w_ref, out_ref):
    attend(mixed_ref[...], w_ref, out_ref)


def second_kernel(own_ref, near_ref, far_ref, w_ref, base_ref, ids_ref, out_ref, other):
    exact = own_ref[...] + near_ref[...] + far_ref[...].astype(jnp.float32)
    attend(split(exact), w_ref, other)
    mask = jnp.concatenate(
        [
            ids_ref[b, 2:3, :].astype(jnp.float32) for b in range(ids_ref.shape[0])
        ],
        axis=1,
    )
    difference = (base_ref[...] - other[...]).astype(jnp.bfloat16)
    kept = (difference.astype(jnp.float32) * mask).astype(jnp.bfloat16)
    gram = lax.dot_general(
        kept, difference, (((1,), (1,)), ((), ())), preferred_element_type=jnp.float32
    )
    count = jnp.sum(mask, axis=1, keepdims=True)
    out_ref[...] = gram / jnp.maximum(count, 1.0)


def attention_cost(length, head_dim):
    return pl.CostEstimate(
        flops=4 * length * length * head_dim,
        bytes_accessed=2 * 1024 * 1024,
        transcendentals=length * length // 2,
    )


def attend_first(mixed, w_head):
    head_dim, length = mixed.shape[0] // 2, mixed.shape[1]
    return pl.pallas_call(
        first_kernel,
        out_shape=jax.ShapeDtypeStruct((head_dim, length), jnp.float32),
        in_specs=[WHOLE] * 2,
        out_specs=WHOLE,
        compiler_params=params(),
        cost_estimate=attention_cost(length, head_dim),
    )(mixed, w_head)


def attend_second(own, near, far, w_head, base, ids):
    head_dim, length = own.shape
    return pl.pallas_call(
        second_kernel,
        out_shape=jax.ShapeDtypeStruct((head_dim, head_dim), jnp.float32),
        in_specs=[WHOLE] * 6,
        out_specs=WHOLE,
        scratch_shapes=[pltpu.VMEM((head_dim, length), jnp.float32)],
        compiler_params=params(),
        cost_estimate=attention_cost(length, head_dim),
    )(own, near, far, w_head, base, ids)


def body(token_ids, pair_mask, embed_table, conv_filter, w_out, w_qkv):
    seq_count, mp_count = lax.axis_size("seq"), lax.axis_size("mp")
    channels = embed_table.shape[2]
    filters, taps = conv_filter.shape
    group = channels // filters
    local_heads, head_dim = w_qkv.shape[1], w_qkv.shape[2]
    sharers = seq_count // local_heads
    assert sharers * local_heads == seq_count
    assert mp_count == 4
    assert token_ids.shape[1] % taps == 0

    packed = jnp.concatenate([token_ids, pair_mask[None]], 0)
    table, weight = make_tables(
        (0, 1, 2, 3),
        seq_count,
        local_heads,
        head_dim,
        jnp.transpose(embed_table, (1, 0, 2)),
        w_out,
    )
    (table, weight), conv_filter = lax.optimization_barrier(((table, weight), conv_filter))
    toeplitz = make_toeplitz(conv_filter)
    ids = gather_small(packed, "seq")
    w_head = lax.dynamic_slice_in_dim(w_qkv, head_here(seq_count, local_heads), 1, 1)
    blocks_here = token_ids.shape[1] // taps
    if blocks_here > 1:
        ids = ids.reshape(seq_count, 3, blocks_here, taps).transpose(0, 2, 1, 3)
        ids = ids.reshape(seq_count * blocks_here, 3, taps)

    mixed0, passed0, diagonal0 = hyena(0, group, ids, table, toeplitz, weight, conv_filter)
    diagonal0 = swap(diagonal0, "mp", 1)
    own0, near0 = project(mixed0, weight, taps, conv_filter)
    total0 = add_parts(passed0, diagonal0, own0)
    near0 = swap(near0, "mp", 1)
    far0 = swap(total0, "mp", 2)
    mixed1, passed1, diagonal1 = hyena(1, group, ids, table, toeplitz, weight, total0)
    diagonal1 = swap(diagonal1, "mp", 1)
    complete0 = complete(own0, near0, far0)
    total1 = add_parts(passed1, diagonal1, complete0)
    far1 = swap(total1, "mp", 2)
    own1, near1 = project(mixed1, weight, taps, total1)
    near1 = swap(near1, "mp", 1)
    base = attend_first(complete0, w_head)
    gram = attend_second(own1, near1, far1, w_head, base, ids)
    rows = lax.all_to_all(gram, "seq", 0, 0, tiled=True)
    rows = rows.reshape(local_heads, sharers, head_dim // seq_count, head_dim)
    return rows[:, 0]


def solution(mesh):
    in_specs = (
        P(None, "seq"),
        P("seq"),
        P(None, None, "mp"),
        P("mp", None),
        P("mp", None),
        P(None, "mp", None, None),
    )
    out_specs = P("mp", "seq", None)
    return jax.shard_map(body, mesh=mesh, in_specs=in_specs, out_specs=out_specs, check_vma=False)
```

```python
import functools
import math

import jax
import jax.numpy as jnp
from jax import lax
from jax.experimental import pallas as pl
from jax.experimental.pallas import tpu as pltpu
from jax.sharding import PartitionSpec as P

MASKED_SCORE = -1e30
VMEM_BYTES = 24 * 1024 * 1024
TABLES_VMEM_BYTES = 48 * 1024 * 1024
WHOLE = pl.BlockSpec(memory_space=pltpu.VMEM)
IN_HBM = pl.BlockSpec(memory_space=pltpu.HBM)


def params(limit=VMEM_BYTES):
    return pltpu.CompilerParams(vmem_limit_bytes=limit)


def bits_of(count):
    width = count.bit_length() - 1
    assert 1 << width == count
    return width


def swap(value, axis, turn):
    count = lax.axis_size(axis)
    return lax.ppermute(value, axis, [(i, i ^ turn) for i in range(count)])


def gather_small(block, axis):
    index = lax.axis_index(axis)
    held = block[None]
    bits = list(range(bits_of(lax.axis_size(axis))))
    for group in [bits[i : i + 2] for i in range(0, len(bits), 2)]:
        pieces = []
        for turn in range(1 << len(group)):
            mask = turn << group[0]
            pieces.append(held if turn == 0 else swap(held, axis, mask))
        for place, bit in enumerate(group):
            upper = ((index >> bit) & 1) == 1
            pieces = [
                jnp.where(upper, pieces[turn ^ (1 << place)], pieces[turn])
                for turn in range(len(pieces))
            ]
        held = jnp.concatenate(pieces, 0)
    return held


def head_here(seq_count, local_heads):
    return lax.axis_index("seq") // (seq_count // local_heads)


def tables_kernel(
    order, local_heads, seq_count, head_dim, embed_ref, w_out_ref, table_ref, weight_ref, planes,
    columns, plane_sems, column_sems
):
    _, vocab, channels = embed_ref.shape
    chunk = planes.shape[2]
    head = head_here(seq_count, local_heads)
    mp_index = lax.axis_index("mp")
    plane_copies = []
    for c in range(vocab // chunk):
        rows = pl.ds(c * chunk, chunk)
        plane_copies.append(
            [
                pltpu.make_async_copy(embed_ref.at[i, rows], planes.at[i, c], plane_sems.at[i, c])
                for i in range(3)
            ]
        )
    column_copies = []
    for p, turn in enumerate(order):
        first = pl.multiple_of(((mp_index ^ turn) * local_heads + head) * head_dim, head_dim)
        column_copies.append(
            pltpu.make_async_copy(
                w_out_ref.at[:, pl.ds(first, head_dim)], columns.at[p], column_sems.at[p]
            )
        )
    for copy in column_copies:
        copy.start()
    for trio in plane_copies:
        for copy in trio:
            copy.start()
    for p, copy in enumerate(column_copies):
        copy.wait()
        weight_ref[p * head_dim : (p + 1) * head_dim, :] = columns[p].T
    for c, trio in enumerate(plane_copies):
        for copy in trio:
            copy.wait()
        cols = slice(c * chunk, (c + 1) * chunk)
        gated = planes[1, c].astype(jnp.float32) * planes[2, c].astype(jnp.float32)
        table_ref[0:channels, cols] = gated.astype(jnp.bfloat16).T
        table_ref[channels : 2 * channels, cols] = planes[0, c].T


def make_tables(order, seq_count, local_heads, head_dim, embed_rows, w_out):
    _, vocab, channels = embed_rows.shape
    count = len(order)
    chunk = 128
    return pl.pallas_call(
        functools.partial(tables_kernel, order, local_heads, seq_count, head_dim),
        out_shape=[
            jax.ShapeDtypeStruct((2 * channels, vocab), jnp.bfloat16),
            jax.ShapeDtypeStruct((count * head_dim, w_out.shape[0]), jnp.bfloat16),
        ],
        in_specs=[IN_HBM, IN_HBM],
        out_specs=[WHOLE] * 2,
        scratch_shapes=[
            pltpu.VMEM((3, vocab // chunk, chunk, channels), jnp.bfloat16),
            pltpu.VMEM((count, w_out.shape[0], head_dim), jnp.bfloat16),
            pltpu.SemaphoreType.DMA((3, vocab // chunk)),
            pltpu.SemaphoreType.DMA((count,)),
        ],
        compiler_params=params(TABLES_VMEM_BYTES),
        cost_estimate=pl.CostEstimate(
            flops=4 * vocab * channels, bytes_accessed=8 * 1024 * 1024, transcendentals=0
        ),
    )(embed_rows, w_out)


def toeplitz_kernel(filter_ref, toeplitz_ref):
    filters, taps = filter_ref.shape
    row = lax.broadcasted_iota(jnp.int32, (taps, taps), 0)
    col = lax.broadcasted_iota(jnp.int32, (taps, taps), 1)
    for g in range(filters):
        spread = jnp.broadcast_to(filter_ref[g : g + 1, :].astype(jnp.float32), (taps, taps))
        rolled = pltpu.roll(spread, 0, 1, stride=1, stride_axis=0)
        toeplitz_ref[g, 0:taps, :] = jnp.where(col < row, rolled, 0.0).astype(jnp.bfloat16)
        toeplitz_ref[g, taps : 2 * taps, :] = jnp.where(col >= row, rolled, 0.0).astype(
            jnp.bfloat16
        )


def make_toeplitz(conv_filter):
    filters, taps = conv_filter.shape
    return pl.pallas_call(
        toeplitz_kernel,
        out_shape=jax.ShapeDtypeStruct((filters, 2 * taps, taps), jnp.bfloat16),
        in_specs=[WHOLE],
        out_specs=WHOLE,
        compiler_params=params(),
        cost_estimate=pl.CostEstimate(
            flops=4 * filters * taps * taps,
            bytes_accessed=4 * filters * taps * taps,
            transcendentals=0,
        ),
    )(conv_filter)


def hyena_kernel(
    which,
    group,
    ids_ref,
    table_ref,
    toeplitz_ref,
    weight_ref,
    _,
    out_ref,
    pass_ref,
    send_ref,
    feat,
    last,
):
    taps = ids_ref.shape[2]
    channels2, vocab = table_ref.shape
    channels = channels2 // 2
    filters = toeplitz_ref.shape[0]
    blocks = feat.shape[1] // taps
    step_index = pl.program_id(0)

    @pl.when(step_index == 0)
    def _():
        last[...] = jnp.zeros_like(last)

    entry = lax.broadcasted_iota(jnp.int32, (vocab, taps), 0)
    step = 2 if blocks % 2 == 0 else 1
    for b in range(0, blocks, step):
        hot = []
        for j in range(step):
            place = step_index * blocks + b + j
            tokens = jnp.broadcast_to(ids_ref[place, which : which + 1, :], (vocab, taps))
            hot.append((entry == tokens).astype(jnp.float32).astype(jnp.bfloat16))
        feat[:, b * taps : (b + step) * taps] = jnp.dot(
            table_ref[...], jnp.concatenate(hot, axis=1), preferred_element_type=jnp.float32
        ).astype(jnp.bfloat16)

    for g in range(filters):
        rows = slice(g * group, (g + 1) * group)
        lead_rows = slice(channels + g * group, channels + (g + 1) * group)
        tiles = [last[rows, :]] + [feat[rows, b * taps : (b + 1) * taps] for b in range(blocks)]
        window = jnp.concatenate(
            [jnp.concatenate([tiles[b], tiles[b + 1]], axis=1) for b in range(blocks)], axis=0
        )
        conv = jnp.dot(window, toeplitz_ref[g], preferred_element_type=jnp.float32)
        for b in range(blocks):
            cols = slice(b * taps, (b + 1) * taps)
            out_ref[rows, cols] = (
                feat[lead_rows, cols].astype(jnp.float32) * conv[b * group : (b + 1) * group, :]
            ).astype(jnp.bfloat16)
    last[...] = feat[0:channels, (blocks - 1) * taps :]
    rows = send_ref.shape[0]
    total = jnp.dot(weight_ref[2 * rows :, :], out_ref[...], preferred_element_type=jnp.float32)
    pass_ref[...] = total[0:rows]
    send_ref[...] = total[rows:]


def tiles_of(length, taps):
    tile = min(length, 8 * taps)
    assert length % tile == 0
    return tile, length // tile


def column_specs(length, tile, rows):
    if length == tile:
        return [WHOLE for _ in rows]
    return [pl.BlockSpec((count, tile), lambda i: (0, i)) for count in rows]


def hyena(which, group, ids, table, toeplitz, weight, after):
    taps = ids.shape[2]
    channels = table.shape[0] // 2
    vocab = table.shape[1]
    length = ids.shape[0] * taps
    head_dim = weight.shape[0] // 4
    tile, steps = tiles_of(length, taps)
    return pl.pallas_call(
        functools.partial(hyena_kernel, which, group),
        out_shape=[
            jax.ShapeDtypeStruct((channels, length), jnp.bfloat16),
            jax.ShapeDtypeStruct((head_dim, length), jnp.float32),
            jax.ShapeDtypeStruct((head_dim, length), jnp.float32),
        ],
        grid=(steps,),
        in_specs=[WHOLE] * 5,
        out_specs=column_specs(length, tile, (channels, head_dim, head_dim)),
        scratch_shapes=[
            pltpu.VMEM((2 * channels, tile), jnp.bfloat16),
            pltpu.VMEM((channels, taps), jnp.bfloat16),
        ],
        compiler_params=params(),
        cost_estimate=pl.CostEstimate(
            flops=4 * length * channels * (vocab + taps) + 4 * length * channels * head_dim,
            bytes_accessed=8 * 1024 * 1024,
            transcendentals=0,
        ),
    )(ids, table, toeplitz, weight, after)


def project_kernel(mixed_ref, weight_ref, _, own_ref, near_ref):
    rows = own_ref.shape[0]
    total = jnp.dot(
        weight_ref[0 : 2 * rows, :], mixed_ref[...], preferred_element_type=jnp.float32
    )
    own_ref[...] = total[0:rows]
    near_ref[...] = total[rows:]


def project(mixed, weight, taps, after):
    channels, length = mixed.shape
    rows = weight.shape[0] // 4
    tile, steps = tiles_of(length, taps)
    specs = column_specs(length, tile, (channels, rows, rows))
    return pl.pallas_call(
        project_kernel,
        out_shape=[jax.ShapeDtypeStruct((rows, length), jnp.float32)] * 2,
        grid=(steps,),
        in_specs=[specs[0], WHOLE, WHOLE],
        out_specs=specs[1:],
        compiler_params=params(),
        cost_estimate=pl.CostEstimate(
            flops=4 * length * channels * rows, bytes_accessed=1024 * 1024, transcendentals=0
        ),
    )(mixed, weight, after)


def split(exact):
    upper = exact.astype(jnp.bfloat16)
    lower = (exact - upper.astype(jnp.float32)).astype(jnp.bfloat16)
    return jnp.concatenate([upper, lower], axis=0)


def add_kernel(mine_ref, theirs_ref, *refs):
    out_ref = refs[-1]
    out_ref[...] = (mine_ref[...] + theirs_ref[...]).astype(out_ref.dtype)


def complete_kernel(own_ref, near_ref, far_ref, mixed_ref):
    mixed_ref[...] = split(own_ref[...] + near_ref[...] + far_ref[...].astype(jnp.float32))


def add_parts(mine, theirs, after):
    return pl.pallas_call(
        add_kernel,
        out_shape=jax.ShapeDtypeStruct(mine.shape, jnp.bfloat16),
        in_specs=[WHOLE] * (2 + len(after)),
        out_specs=WHOLE,
        compiler_params=params(),
        cost_estimate=pl.CostEstimate(
            flops=mine.size, bytes_accessed=10 * mine.size, transcendentals=0
        ),
    )(mine, theirs, *after)


def complete(own, near, far):
    rows, length = own.shape
    return pl.pallas_call(
        complete_kernel,
        out_shape=jax.ShapeDtypeStruct((2 * rows, length), jnp.bfloat16),
        in_specs=[WHOLE] * 3,
        out_specs=WHOLE,
        compiler_params=params(),
        cost_estimate=pl.CostEstimate(
            flops=40000 * own.size, bytes_accessed=14 * own.size, transcendentals=0
        ),
    )(own, near, far)


def attend(mixed, w_ref, out_ref):
    head_dim, length = out_ref.shape
    scale = math.log2(math.e) / math.sqrt(head_dim)

    def project_head(which):
        weight = w_ref[which, 0].T
        return jnp.dot(
            jnp.concatenate([weight, weight], axis=1), mixed, preferred_element_type=jnp.float32
        ).astype(jnp.bfloat16)

    queries, keys, values = project_head(0), project_head(1).T, project_head(2)

    def finish(first, parts, values_seen):
        top = functools.reduce(
            jnp.maximum, [jnp.max(part, axis=0, keepdims=True) for part in parts]
        )
        weights = [jnp.exp2((part - top) * scale) for part in parts]
        row_sum = sum(jnp.sum(part, axis=0, keepdims=True) for part in weights)
        probs = jnp.concatenate([part.astype(jnp.bfloat16) for part in weights], axis=0)
        return jnp.dot(values_seen, probs, preferred_element_type=jnp.float32) / row_sum

    def score(keys_seen, queries_block):
        return jnp.dot(keys_seen, queries_block, preferred_element_type=jnp.float32)

    if length <= 2048:
        span = min(512, length)
        row = lax.broadcasted_iota(jnp.int32, (span, span), 0)
        col = lax.broadcasted_iota(jnp.int32, (span, span), 1)
        for first in range(0, length, span):
            cols = slice(first, first + span)
            parts = [jnp.where(row <= col, score(keys[cols], queries[:, cols]), MASKED_SCORE)]
            if first > 0:
                parts = [score(keys[:first], queries[:, cols])] + parts
            out_ref[:, cols] = finish(first, parts, values[:, : first + span])
    else:
        span = 256
        out_ref[...] = queries.astype(jnp.float32)

        @pl.loop(0, length // span)
        def _(i):
            first = pl.multiple_of(i * span, span)
            cols = pl.ds(first, span)
            scores = score(keys, out_ref[:, cols].astype(jnp.bfloat16))
            key_pos = lax.broadcasted_iota(jnp.int32, scores.shape, 0)
            query_pos = first + lax.broadcasted_iota(jnp.int32, scores.shape, 1)
            scores = jnp.where(key_pos <= query_pos, scores, MASKED_SCORE)
            out_ref[:, cols] = finish(first, [scores], values)


def first_kernel(mixed_ref, w_ref, out_ref):
    attend(mixed_ref[...], w_ref, out_ref)


def second_kernel(own_ref, near_ref, far_ref, w_ref, base_ref, ids_ref, out_ref, other):
    exact = own_ref[...] + near_ref[...] + far_ref[...].astype(jnp.float32)
    attend(split(exact), w_ref, other)
    mask = jnp.concatenate(
        [
            ids_ref[b, 2:3, :].astype(jnp.float32) for b in range(ids_ref.shape[0])
        ],
        axis=1,
    )
    difference = (base_ref[...] - other[...]).astype(jnp.bfloat16)
    kept = (difference.astype(jnp.float32) * mask).astype(jnp.bfloat16)
    gram = lax.dot_general(
        kept, difference, (((1,), (1,)), ((), ())), preferred_element_type=jnp.float32
    )
    count = jnp.sum(mask, axis=1, keepdims=True)
    out_ref[...] = gram / jnp.maximum(count, 1.0)


def attention_cost(length, head_dim):
    return pl.CostEstimate(
        flops=4 * length * length * head_dim,
        bytes_accessed=2 * 1024 * 1024,
        transcendentals=length * length // 2,
    )


def attend_first(mixed, w_head):
    head_dim, length = mixed.shape[0] // 2, mixed.shape[1]
    return pl.pallas_call(
        first_kernel,
        out_shape=jax.ShapeDtypeStruct((head_dim, length), jnp.float32),
        in_specs=[WHOLE] * 2,
        out_specs=WHOLE,
        compiler_params=params(),
        cost_estimate=attention_cost(length, head_dim),
    )(mixed, w_head)


def attend_second(own, near, far, w_head, base, ids):
    head_dim, length = own.shape
    return pl.pallas_call(
        second_kernel,
        out_shape=jax.ShapeDtypeStruct((head_dim, head_dim), jnp.float32),
        in_specs=[WHOLE] * 6,
        out_specs=WHOLE,
        scratch_shapes=[pltpu.VMEM((head_dim, length), jnp.float32)],
        compiler_params=params(),
        cost_estimate=attention_cost(length, head_dim),
    )(own, near, far, w_head, base, ids)


def body(token_ids, pair_mask, embed_table, conv_filter, w_out, w_qkv):
    seq_count, mp_count = lax.axis_size("seq"), lax.axis_size("mp")
    channels = embed_table.shape[2]
    filters, taps = conv_filter.shape
    group = channels // filters
    local_heads, head_dim = w_qkv.shape[1], w_qkv.shape[2]
    sharers = seq_count // local_heads
    assert sharers * local_heads == seq_count
    assert mp_count == 4
    assert token_ids.shape[1] % taps == 0

    packed = jnp.concatenate([token_ids, pair_mask[None]], 0)
    table, weight = make_tables(
        (0, 1, 2, 3),
        seq_count,
        local_heads,
        head_dim,
        jnp.transpose(embed_table, (1, 0, 2)),
        w_out,
    )
    (table, weight), conv_filter = lax.optimization_barrier(((table, weight), conv_filter))
    toeplitz = make_toeplitz(conv_filter)
    ids = gather_small(packed, "seq")
    w_head = lax.dynamic_slice_in_dim(w_qkv, head_here(seq_count, local_heads), 1, 1)
    blocks_here = token_ids.shape[1] // taps
    if blocks_here > 1:
        ids = ids.reshape(seq_count, 3, blocks_here, taps).transpose(0, 2, 1, 3)
        ids = ids.reshape(seq_count * blocks_here, 3, taps)

    mixed0, passed0, diagonal0 = hyena(0, group, ids, table, toeplitz, weight, conv_filter)
    diagonal0 = swap(diagonal0, "mp", 1)
    own0, near0 = project(mixed0, weight, taps, conv_filter)
    total0 = add_parts(passed0, diagonal0, [own0])
    near0 = swap(near0, "mp", 1)
    far0 = swap(total0, "mp", 2)
    mixed1, passed1, diagonal1 = hyena(1, group, ids, table, toeplitz, weight, total0)
    diagonal1 = swap(diagonal1, "mp", 1)
    own1, near1 = project(mixed1, weight, taps, conv_filter)
    complete0 = complete(own0, near0, far0)
    total1 = add_parts(passed1, diagonal1, [complete0, own1])
    near1 = swap(near1, "mp", 1)
    far1 = swap(total1, "mp", 2)
    base = attend_first(complete0, w_head)
    gram = attend_second(own1, near1, far1, w_head, base, ids)
    rows = lax.all_to_all(gram, "seq", 0, 0, tiled=True)
    rows = rows.reshape(local_heads, sharers, head_dim // seq_count, head_dim)
    return rows[:, 0]


def solution(mesh):
    in_specs = (
        P(None, "seq"),
        P("seq"),
        P(None, None, "mp"),
        P("mp", None),
        P("mp", None),
        P(None, "mp", None, None),
    )
    out_specs = P("mp", "seq", None)
    return jax.shard_map(body, mesh=mesh, in_specs=in_specs, out_specs=out_specs, check_vma=False)
```

```python
import functools
import math

import jax
import jax.numpy as jnp
from jax import lax
from jax.experimental import pallas as pl
from jax.experimental.pallas import tpu as pltpu
from jax.sharding import PartitionSpec as P

MASKED_SCORE = -1e30
VMEM_BYTES = 24 * 1024 * 1024
TABLES_VMEM_BYTES = 49 * 1024 * 1024
WEIGHTS_VMEM_BYTES = 50 * 1024 * 1024
WHOLE = pl.BlockSpec(memory_space=pltpu.VMEM)
IN_HBM = pl.BlockSpec(memory_space=pltpu.HBM)


def params(limit=VMEM_BYTES):
    return pltpu.CompilerParams(vmem_limit_bytes=limit)


def bits_of(count):
    width = count.bit_length() - 1
    assert 1 << width == count
    return width


def swap(value, axis, turn):
    count = lax.axis_size(axis)
    return lax.ppermute(value, axis, [(i, i ^ turn) for i in range(count)])


def gather_small(block, axis, zeros):
    index = lax.axis_index(axis)
    held = block[None]
    bits = list(range(bits_of(lax.axis_size(axis))))
    bits = bits[1:] + bits[:1]
    seen = []
    for group in [bits[i : i + 2] for i in range(0, len(bits), 2)]:
        pieces = []
        for turn in range(1 << len(group)):
            mask = sum(((turn >> place) & 1) << bit for place, bit in enumerate(group))
            pieces.append(held if turn == 0 else swap(held, axis, mask))
        if not seen:
            pieces = [piece + zeros for piece in pieces]
        for place, bit in enumerate(group):
            upper = ((index >> bit) & 1) == 1
            pieces = [
                jnp.where(upper, pieces[turn ^ (1 << place)], pieces[turn])
                for turn in range(len(pieces))
            ]
        held = jnp.concatenate(pieces, 0)
        seen = group[::-1] + seen
    tail = held.shape[1:]
    held = held.reshape([2] * len(bits) + list(tail))
    order = [seen.index(bit) for bit in sorted(bits, reverse=True)]
    held = held.transpose(order + [len(bits) + d for d in range(len(tail))])
    return held.reshape((-1,) + tail)


def head_here(seq_count, local_heads):
    return lax.axis_index("seq") // (seq_count // local_heads)


def tables_kernel(embed_ref, table_ref, planes, sems):
    _, vocab, channels = embed_ref.shape
    chunk = planes.shape[2]
    copies = []
    for c in range(vocab // chunk):
        rows = pl.ds(c * chunk, chunk)
        copies.append(
            [
                pltpu.make_async_copy(embed_ref.at[i, rows], planes.at[i, c], sems.at[i, c])
                for i in range(3)
            ]
        )
        for copy in copies[-1]:
            copy.start()
    for c, trio in enumerate(copies):
        for copy in trio:
            copy.wait()
        cols = slice(c * chunk, (c + 1) * chunk)
        gated = planes[1, c].astype(jnp.float32) * planes[2, c].astype(jnp.float32)
        table_ref[0:channels, cols] = gated.astype(jnp.bfloat16).T
        table_ref[channels : 2 * channels, cols] = planes[0, c].T


def make_tables(embed_rows):
    _, vocab, channels = embed_rows.shape
    chunk = 128
    return pl.pallas_call(
        tables_kernel,
        out_shape=jax.ShapeDtypeStruct((2 * channels, vocab), jnp.bfloat16),
        in_specs=[IN_HBM],
        out_specs=WHOLE,
        scratch_shapes=[
            pltpu.VMEM((3, vocab // chunk, chunk, channels), jnp.bfloat16),
            pltpu.SemaphoreType.DMA((3, vocab // chunk)),
        ],
        compiler_params=params(TABLES_VMEM_BYTES),
        cost_estimate=pl.CostEstimate(
            flops=4 * vocab * channels, bytes_accessed=8 * 1024 * 1024, transcendentals=0
        ),
    )(embed_rows)


def weights_kernel(
    order, local_heads, seq_count, head_dim, w_out_ref, weight_ref, zeros_ref, columns, sems
):
    head = head_here(seq_count, local_heads)
    mp_index = lax.axis_index("mp")
    copies = []
    for p, turn in enumerate(order):
        first = pl.multiple_of(((mp_index ^ turn) * local_heads + head) * head_dim, head_dim)
        copies.append(
            pltpu.make_async_copy(
                w_out_ref.at[:, pl.ds(first, head_dim)], columns.at[p], sems.at[p]
            )
        )
    for copy in copies:
        copy.start()
    zeros_ref[...] = jnp.zeros_like(zeros_ref)
    for p, copy in enumerate(copies):
        copy.wait()
        weight_ref[p * head_dim : (p + 1) * head_dim, :] = columns[p].T


def make_weights(order, seq_count, local_heads, head_dim, w_out, ids_shape):
    count = len(order)
    return pl.pallas_call(
        functools.partial(weights_kernel, order, local_heads, seq_count, head_dim),
        out_shape=[
            jax.ShapeDtypeStruct((count * head_dim, w_out.shape[0]), jnp.bfloat16),
            jax.ShapeDtypeStruct(ids_shape, jnp.int32),
        ],
        in_specs=[IN_HBM],
        out_specs=[WHOLE] * 2,
        scratch_shapes=[
            pltpu.VMEM((count, w_out.shape[0], head_dim), jnp.bfloat16),
            pltpu.SemaphoreType.DMA((count,)),
        ],
        compiler_params=params(WEIGHTS_VMEM_BYTES),
        cost_estimate=pl.CostEstimate(
            flops=count * head_dim, bytes_accessed=2 * 1024 * 1024, transcendentals=0
        ),
    )(w_out)


def toeplitz_kernel(filter_ref, toeplitz_ref):
    filters, taps = filter_ref.shape
    row = lax.broadcasted_iota(jnp.int32, (taps, taps), 0)
    col = lax.broadcasted_iota(jnp.int32, (taps, taps), 1)
    for g in range(filters):
        spread = jnp.broadcast_to(filter_ref[g : g + 1, :].astype(jnp.float32), (taps, taps))
        rolled = pltpu.roll(spread, 0, 1, stride=1, stride_axis=0)
        toeplitz_ref[g, 0:taps, :] = jnp.where(col < row, rolled, 0.0).astype(jnp.bfloat16)
        toeplitz_ref[g, taps : 2 * taps, :] = jnp.where(col >= row, rolled, 0.0).astype(
            jnp.bfloat16
        )


def make_toeplitz(conv_filter):
    filters, taps = conv_filter.shape
    return pl.pallas_call(
        toeplitz_kernel,
        out_shape=jax.ShapeDtypeStruct((filters, 2 * taps, taps), jnp.bfloat16),
        in_specs=[WHOLE],
        out_specs=WHOLE,
        compiler_params=params(),
        cost_estimate=pl.CostEstimate(
            flops=4 * filters * taps * taps,
            bytes_accessed=4 * filters * taps * taps,
            transcendentals=0,
        ),
    )(conv_filter)


def hyena_kernel(
    which,
    group,
    ids_ref,
    table_ref,
    toeplitz_ref,
    weight_ref,
    _,
    out_ref,
    send_ref,
    feat,
    last,
):
    taps = ids_ref.shape[2]
    channels2, vocab = table_ref.shape
    channels = channels2 // 2
    filters = toeplitz_ref.shape[0]
    blocks = feat.shape[1] // taps
    step_index = pl.program_id(0)

    @pl.when(step_index == 0)
    def _():
        last[...] = jnp.zeros_like(last)

    entry = lax.broadcasted_iota(jnp.int32, (vocab, taps), 0)
    step = 2 if blocks % 2 == 0 else 1
    for b in range(0, blocks, step):
        hot = []
        for j in range(step):
            place = step_index * blocks + b + j
            tokens = jnp.broadcast_to(ids_ref[place, which : which + 1, :], (vocab, taps))
            hot.append((entry == tokens).astype(jnp.float32).astype(jnp.bfloat16))
        feat[:, b * taps : (b + step) * taps] = jnp.dot(
            table_ref[...], jnp.concatenate(hot, axis=1), preferred_element_type=jnp.float32
        ).astype(jnp.bfloat16)

    for g in range(filters):
        rows = slice(g * group, (g + 1) * group)
        lead_rows = slice(channels + g * group, channels + (g + 1) * group)
        tiles = [last[rows, :]] + [feat[rows, b * taps : (b + 1) * taps] for b in range(blocks)]
        window = jnp.concatenate(
            [jnp.concatenate([tiles[b], tiles[b + 1]], axis=1) for b in range(blocks)], axis=0
        )
        conv = jnp.dot(window, toeplitz_ref[g], preferred_element_type=jnp.float32)
        for b in range(blocks):
            cols = slice(b * taps, (b + 1) * taps)
            out_ref[rows, cols] = (
                feat[lead_rows, cols].astype(jnp.float32) * conv[b * group : (b + 1) * group, :]
            ).astype(jnp.bfloat16)
    last[...] = feat[0:channels, (blocks - 1) * taps :]
    rows = send_ref.shape[0]
    send_ref[...] = jnp.dot(
        weight_ref[3 * rows :, :], out_ref[...], preferred_element_type=jnp.float32
    )


def tiles_of(length, taps):
    tile = min(length, 8 * taps)
    assert length % tile == 0
    return tile, length // tile


def column_specs(length, tile, rows):
    if length == tile:
        return [WHOLE for _ in rows]
    return [pl.BlockSpec((count, tile), lambda i: (0, i)) for count in rows]


def hyena(which, group, ids, table, toeplitz, weight, after):
    taps = ids.shape[2]
    channels = table.shape[0] // 2
    vocab = table.shape[1]
    length = ids.shape[0] * taps
    head_dim = weight.shape[0] // 4
    tile, steps = tiles_of(length, taps)
    return pl.pallas_call(
        functools.partial(hyena_kernel, which, group),
        out_shape=[
            jax.ShapeDtypeStruct((channels, length), jnp.bfloat16),
            jax.ShapeDtypeStruct((head_dim, length), jnp.float32),
        ],
        grid=(steps,),
        in_specs=[WHOLE] * 5,
        out_specs=column_specs(length, tile, (channels, head_dim)),
        scratch_shapes=[
            pltpu.VMEM((2 * channels, tile), jnp.bfloat16),
            pltpu.VMEM((channels, taps), jnp.bfloat16),
        ],
        compiler_params=params(),
        cost_estimate=pl.CostEstimate(
            flops=4 * length * channels * (vocab + taps) + 2 * length * channels * head_dim,
            bytes_accessed=8 * 1024 * 1024,
            transcendentals=0,
        ),
    )(ids, table, toeplitz, weight, after)


def project_kernel(mixed_ref, weight_ref, own_ref, near_ref, pass_ref):
    rows = own_ref.shape[0]
    total = jnp.dot(
        weight_ref[0 : 3 * rows, :], mixed_ref[...], preferred_element_type=jnp.float32
    )
    own_ref[...] = total[0:rows]
    near_ref[...] = total[rows : 2 * rows]
    pass_ref[...] = total[2 * rows :]


def project(mixed, weight, taps):
    channels, length = mixed.shape
    rows = weight.shape[0] // 4
    tile, steps = tiles_of(length, taps)
    specs = column_specs(length, tile, (channels, rows, rows, rows))
    return pl.pallas_call(
        project_kernel,
        out_shape=[jax.ShapeDtypeStruct((rows, length), jnp.float32)] * 3,
        grid=(steps,),
        in_specs=[specs[0], WHOLE],
        out_specs=specs[1:],
        compiler_params=params(),
        cost_estimate=pl.CostEstimate(
            flops=6 * length * channels * rows, bytes_accessed=1024 * 1024, transcendentals=0
        ),
    )(mixed, weight)


def split(exact):
    upper = exact.astype(jnp.bfloat16)
    lower = (exact - upper.astype(jnp.float32)).astype(jnp.bfloat16)
    return jnp.concatenate([upper, lower], axis=0)


def add_kernel(mine_ref, theirs_ref, *refs):
    out_ref = refs[-1]
    out_ref[...] = (mine_ref[...] + theirs_ref[...]).astype(out_ref.dtype)


def complete_kernel(own_ref, near_ref, far_ref, mixed_ref):
    mixed_ref[...] = split(own_ref[...] + near_ref[...] + far_ref[...].astype(jnp.float32))


def add_parts(mine, theirs, after):
    return pl.pallas_call(
        add_kernel,
        out_shape=jax.ShapeDtypeStruct(mine.shape, jnp.bfloat16),
        in_specs=[WHOLE] * (2 + len(after)),
        out_specs=WHOLE,
        compiler_params=params(),
        cost_estimate=pl.CostEstimate(
            flops=mine.size, bytes_accessed=10 * mine.size, transcendentals=0
        ),
    )(mine, theirs, *after)


def complete(own, near, far):
    rows, length = own.shape
    return pl.pallas_call(
        complete_kernel,
        out_shape=jax.ShapeDtypeStruct((2 * rows, length), jnp.bfloat16),
        in_specs=[WHOLE] * 3,
        out_specs=WHOLE,
        compiler_params=params(),
        cost_estimate=pl.CostEstimate(
            flops=40000 * own.size, bytes_accessed=14 * own.size, transcendentals=0
        ),
    )(own, near, far)


def attend(mixed, w_ref, out_ref):
    head_dim, length = out_ref.shape
    scale = math.log2(math.e) / math.sqrt(head_dim)

    def project_head(which):
        weight = w_ref[which, 0].T
        return jnp.dot(
            jnp.concatenate([weight, weight], axis=1), mixed, preferred_element_type=jnp.float32
        ).astype(jnp.bfloat16)

    queries, keys, values = project_head(0), project_head(1).T, project_head(2)

    def softmax(parts):
        top = functools.reduce(
            jnp.maximum, [jnp.max(part, axis=0, keepdims=True) for part in parts]
        )
        weights = [jnp.exp2((part - top) * scale) for part in parts]
        row_sum = sum(jnp.sum(part, axis=0, keepdims=True) for part in weights)
        return jnp.concatenate([part.astype(jnp.bfloat16) for part in weights], axis=0), row_sum

    def score(keys_seen, queries_block):
        return jnp.dot(keys_seen, queries_block, preferred_element_type=jnp.float32)

    def average(values_seen, probs, row_sum):
        total = jnp.dot(values_seen, probs, preferred_element_type=jnp.float32)
        return total * (1.0 / row_sum)

    span = min(256, length)
    if length <= 1024:
        row = lax.broadcasted_iota(jnp.int32, (span, span), 0)
        col = lax.broadcasted_iota(jnp.int32, (span, span), 1)
        scores = []
        for first in range(0, length, span):
            cols = slice(first, first + span)
            parts = [jnp.where(row <= col, score(keys[cols], queries[:, cols]), MASKED_SCORE)]
            if first > 0:
                parts = [score(keys[:first], queries[:, cols])] + parts
            scores.append(parts)
        weighted = [softmax(parts) for parts in scores]
        for i, (probs, row_sum) in enumerate(weighted):
            seen = (i + 1) * span
            out_ref[:, i * span : seen] = average(values[:, :seen], probs, row_sum)
    else:
        out_ref[...] = queries.astype(jnp.float32)

        @pl.loop(0, length // span)
        def _(i):
            first = pl.multiple_of(i * span, span)
            cols = pl.ds(first, span)
            scores = score(keys, out_ref[:, cols].astype(jnp.bfloat16))
            key_pos = lax.broadcasted_iota(jnp.int32, scores.shape, 0)
            query_pos = first + lax.broadcasted_iota(jnp.int32, scores.shape, 1)
            scores = jnp.where(key_pos <= query_pos, scores, MASKED_SCORE)
            out_ref[:, cols] = average(values, *softmax([scores]))


def first_kernel(mixed_ref, w_ref, out_ref):
    attend(mixed_ref[...], w_ref, out_ref)


def second_kernel(own_ref, near_ref, far_ref, w_ref, base_ref, ids_ref, out_ref, other):
    exact = own_ref[...] + near_ref[...] + far_ref[...].astype(jnp.float32)
    attend(split(exact), w_ref, other)
    mask = jnp.concatenate(
        [
            ids_ref[b, 2:3, :].astype(jnp.float32) for b in range(ids_ref.shape[0])
        ],
        axis=1,
    )
    difference = (base_ref[...] - other[...]).astype(jnp.bfloat16)
    kept = (difference.astype(jnp.float32) * mask).astype(jnp.bfloat16)
    gram = lax.dot_general(
        kept, difference, (((1,), (1,)), ((), ())), preferred_element_type=jnp.float32
    )
    count = jnp.sum(mask, axis=1, keepdims=True)
    out_ref[...] = gram * (1.0 / jnp.maximum(count, 1.0))


def attention_cost(length, head_dim):
    return pl.CostEstimate(
        flops=4 * length * length * head_dim,
        bytes_accessed=2 * 1024 * 1024,
        transcendentals=length * length // 2,
    )


def attend_first(mixed, w_head):
    head_dim, length = mixed.shape[0] // 2, mixed.shape[1]
    return pl.pallas_call(
        first_kernel,
        out_shape=jax.ShapeDtypeStruct((head_dim, length), jnp.float32),
        in_specs=[WHOLE] * 2,
        out_specs=WHOLE,
        compiler_params=params(),
        cost_estimate=attention_cost(length, head_dim),
    )(mixed, w_head)


def attend_second(own, near, far, w_head, base, ids):
    head_dim, length = own.shape
    return pl.pallas_call(
        second_kernel,
        out_shape=jax.ShapeDtypeStruct((head_dim, head_dim), jnp.float32),
        in_specs=[WHOLE] * 6,
        out_specs=WHOLE,
        scratch_shapes=[pltpu.VMEM((head_dim, length), jnp.float32)],
        compiler_params=params(),
        cost_estimate=attention_cost(length, head_dim),
    )(own, near, far, w_head, base, ids)


def body(token_ids, pair_mask, embed_table, conv_filter, w_out, w_qkv):
    seq_count, mp_count = lax.axis_size("seq"), lax.axis_size("mp")
    channels = embed_table.shape[2]
    filters, taps = conv_filter.shape
    group = channels // filters
    local_heads, head_dim = w_qkv.shape[1], w_qkv.shape[2]
    sharers = seq_count // local_heads
    assert sharers * local_heads == seq_count
    assert mp_count == 4
    assert token_ids.shape[1] % taps == 0

    packed = jnp.concatenate([token_ids, pair_mask[None]], 0)
    weight, zeros = make_weights(
        (0, 1, 2, 3), seq_count, local_heads, head_dim, w_out, packed.shape
    )
    table = make_tables(jnp.transpose(embed_table, (1, 0, 2)))
    table, conv_filter = lax.optimization_barrier((table, conv_filter))
    toeplitz = make_toeplitz(conv_filter)
    ids = gather_small(packed, "seq", zeros)
    w_head = lax.dynamic_slice_in_dim(w_qkv, head_here(seq_count, local_heads), 1, 1)
    blocks_here = token_ids.shape[1] // taps
    if blocks_here > 1:
        ids = ids.reshape(seq_count, 3, blocks_here, taps).transpose(0, 2, 1, 3)
        ids = ids.reshape(seq_count * blocks_here, 3, taps)

    mixed0, diagonal0 = hyena(0, group, ids, table, toeplitz, weight, conv_filter)
    diagonal0 = swap(diagonal0, "mp", 1)
    own0, near0, passed0 = project(mixed0, weight, taps)
    total0 = add_parts(passed0, diagonal0, [])
    near0 = swap(near0, "mp", 1)
    far0 = swap(total0, "mp", 2)
    mixed1, diagonal1 = hyena(1, group, ids, table, toeplitz, weight, total0)
    diagonal1 = swap(diagonal1, "mp", 1)
    own1, near1, passed1 = project(mixed1, weight, taps)
    complete0 = complete(own0, near0, far0)
    total1 = add_parts(passed1, diagonal1, [complete0])
    near1 = swap(near1, "mp", 1)
    far1 = swap(total1, "mp", 2)
    base = attend_first(complete0, w_head)
    gram = attend_second(own1, near1, far1, w_head, base, ids)
    rows = lax.all_to_all(gram, "seq", 0, 0, tiled=True)
    rows = rows.reshape(local_heads, sharers, head_dim // seq_count, head_dim)
    return rows[:, 0]


def solution(mesh):
    in_specs = (
        P(None, "seq"),
        P("seq"),
        P(None, None, "mp"),
        P("mp", None),
        P("mp", None),
        P(None, "mp", None, None),
    )
    out_specs = P("mp", "seq", None)
    return jax.shard_map(body, mesh=mesh, in_specs=in_specs, out_specs=out_specs, check_vma=False)
```
